32 devices in a mesh: grp: 2 (over x), tm: 16 (over z, y, core).
Axes of the slice: x: 2, y: 2, z: 4, core: 2. Of those that a mesh axis runs over, the one named last changes fastest.
Arguments:
- signals: bfloat16 [8, 1024, 256], P('grp', 'tm'), parts along dimension 0, may hold values from -6 to 6
- targets: bfloat16 [8, 1024, 768], P('grp', 'tm'), parts along dimension 0, may hold values from -6 to 6
- decay_rate: float32 [4096], P('grp'), parts along dimension 0, may hold values from 0 to 0.125, as said below
- pole_angle: float32 [4096], P('grp'), parts along dimension 0, may hold values from -3.1416 to 3.1416
- in_map: bfloat16 [8192, 256], P('grp'), parts along dimension 0
- out_map: bfloat16 [8192, 768], P('grp'), parts along dimension 0
Outputs:
- out_update: float32 [8192, 768], P(('grp', 'tm')), parts along dimension 0
- in_update: float32 [8192, 256], P(('grp', 'tm')), parts along dimension 0
- boundary_adjoint: float32 [8, 16, 4096], P('grp', 'tm'), parts along dimension 0
The draws below stay inside these ranges and needn't reach their ends.
There are 2 independent parts, one for each index of `grp`. The reference program is written for one: setup_inputs(seed, part) draws one part's arguments, and reference() takes and returns one part's arrays. A program takes and returns all parts, laid end to end along the dimension named above; each array names one. Nothing has to cross between parts.
Inputs may be any that keep to these rules, and one draw needn't show every extreme that they name: Every mode decays: exp(-decay_rate) lies below 1.
All inputs are finite; a program needn't handle non-finite values.
Results may differ from the reference program's by a relative error of at most 0.0027.
Values sent between devices are 32-bit elements; how exact they have to be, the bound alone decides.
A program may use at most 128 MiB of HBM per device.

```python
import math
import jax
import jax.numpy as jnp
from jax import lax

MODES = 2048
SENSORS = 256
TARGETS = 768
MEMBERS = 4
GROUP = 64
STEPS = 1024
N_TM = 16


def mode_draws(key):
    keys = jax.random.split(jax.random.fold_in(key, 101), 7)
    slow_share = 0.4
    mid_share = 0.35
    pick = jax.random.uniform(keys[0], (MODES,), jnp.float32)
    slow_rate = jnp.exp(jax.random.uniform(keys[1], (MODES,), jnp.float32, math.log(0.05), math.log(2.0))) / STEPS
    mid_rate = 1.0 / jax.random.uniform(keys[2], (MODES,), jnp.float32, 52.0, 63.5)
    fast_rate = 1.0 / jax.random.uniform(keys[3], (MODES,), jnp.float32, 8.0, 40.0)
    rate = jnp.where(pick < slow_share, slow_rate, jnp.where(pick < slow_share + mid_share, mid_rate, fast_rate))
    still = jax.random.uniform(keys[4], (MODES,), jnp.float32) < 0.5
    small_turn = rate * jax.random.uniform(keys[5], (MODES,), jnp.float32, -0.3, 0.3)
    full_turn = jax.random.uniform(keys[6], (MODES,), jnp.float32, -math.pi, math.pi)
    turn = jnp.where(still, small_turn, full_turn)
    return (rate.astype(jnp.float32), turn.astype(jnp.float32))


def draw_decay_rate(key, part):
    rate, turn = mode_draws(key)
    return rate


def draw_pole_angle(key, part):
    rate, turn = mode_draws(key)
    return turn


def map_draw(key, salt, height, breadth, fan):
    keys = jax.random.split(jax.random.fold_in(key, salt), 3)
    base = jnp.clip(jax.random.normal(keys[0], (height, breadth), jnp.float32), -6.0, 6.0)
    row_scale = jnp.exp(jax.random.uniform(keys[1], (height, 1), jnp.float32, math.log(0.35), math.log(2.8)))
    imag_scale = jnp.exp(jax.random.uniform(keys[2], (), jnp.float32, math.log(0.15), math.log(0.35)))
    side = jnp.where(jnp.arange(height)[:, None] >= MODES, imag_scale, jnp.float32(1.0))
    return (base * row_scale * side * float(fan) ** (-0.5)).astype(jnp.float32)


def draw_in_map(key, part):
    return map_draw(key, 211, 2 * MODES, SENSORS, SENSORS).astype(jnp.bfloat16)


def draw_out_map(key, part):
    return map_draw(key, 307, 2 * MODES, TARGETS, 2 * MODES).astype(jnp.bfloat16)


def levels(key, extent, cuts, smallest, largest):
    loudness = 1.0
    for position, blocks in cuts:
        draws = jax.random.uniform(jax.random.fold_in(jax.random.fold_in(key, 6), position), (blocks,), jnp.float32, smallest / len(cuts), largest / len(cuts))
        loudness = loudness * jnp.repeat(jnp.exp(draws), extent[position] // blocks).reshape((-1,) + (1,) * (len(extent) - 1 - position))
    return loudness


def normal_values(rng, shape, width, reach, cuts=(), held_as=jnp.bfloat16):
    result = width * jax.random.normal(rng, shape, jnp.float32)
    if cuts:
        result = result * levels(rng, shape, cuts, -0.22, 0.18)
    return jnp.clip(result, -reach, reach).astype(held_as)


def setup_inputs(seed: int = 0, part: int = 0) -> dict:
    streams_of = jax.random.split(jax.random.key(seed), 7)
    part_keys = jax.random.split(jax.random.fold_in(streams_of[6], part), 7)
    return {
        "signals": normal_values(part_keys[0], (MEMBERS, STEPS, SENSORS), 1.0, 6.0, ((1, 16),)),
        "targets": normal_values(part_keys[1], (MEMBERS, STEPS, TARGETS), 1.0, 6.0, ((1, 16),)),
        "decay_rate": draw_decay_rate(jax.random.fold_in(jax.random.fold_in(streams_of[6], part), 71), part),
        "pole_angle": draw_pole_angle(jax.random.fold_in(jax.random.fold_in(streams_of[6], part), 71), part),
        "in_map": draw_in_map(jax.random.fold_in(jax.random.fold_in(streams_of[6], part), 71), part),
        "out_map": draw_out_map(jax.random.fold_in(jax.random.fold_in(streams_of[6], part), 71), part),
    }


def cmul(first, second):
    half = first.shape[-1] // 2
    fr = first[..., :half]
    fi = first[..., half:]
    sr = second[..., :half]
    si = second[..., half:]
    return jnp.concatenate([fr * sr - fi * si, fr * si + fi * sr], axis=-1)

def reference(signals, targets, decay_rate, pole_angle, in_map, out_map):
    magnitude = jnp.exp(-decay_rate)
    step_pair = jnp.concatenate([magnitude * jnp.cos(pole_angle), magnitude * jnp.sin(pole_angle)])
    conj_pair = jnp.concatenate([magnitude * jnp.cos(pole_angle), -magnitude * jnp.sin(pole_angle)])
    gain = jnp.sqrt(-jnp.expm1(-2.0 * decay_rate))
    gain_pair = jnp.concatenate([gain, gain])
    sig_blocks = signals.reshape(MEMBERS, N_TM, GROUP, SENSORS).transpose(1, 0, 2, 3)
    tgt_blocks = targets.reshape(MEMBERS, N_TM, GROUP, TARGETS).transpose(1, 0, 2, 3)

    def forward(carry, block):
        state, grad_out = carry
        sig, tgt = block
        drive = lax.dot_general(sig, in_map, (((2,), (1,)), ((), ())), preferred_element_type=jnp.float32) * gain_pair

        def advance(current, column):
            following = cmul(step_pair, current) + column
            return (following, following)
        state, seq = lax.scan(advance, state, drive.transpose(1, 0, 2))
        states_b = seq.transpose(1, 0, 2).astype(jnp.bfloat16)
        predicted = lax.dot_general(states_b, out_map, (((2,), (0,)), ((), ())), preferred_element_type=jnp.float32)
        misfit_b = (predicted - tgt.astype(jnp.float32)).astype(jnp.bfloat16)
        grad_out = grad_out + lax.dot_general(states_b, misfit_b, (((0, 1), (0, 1)), ((), ())), preferred_element_type=jnp.float32)
        return ((state, grad_out), misfit_b)
    start_state = jnp.zeros((MEMBERS, 2 * MODES), jnp.float32)
    start_out = jnp.zeros((2 * MODES, TARGETS), jnp.float32)
    (last_state, grad_out), misfits = lax.scan(forward, (start_state, start_out), (sig_blocks, tgt_blocks))

    def backward(carry, block):
        adjoint, grad_in = carry
        sig, misfit_b = block
        back = lax.dot_general(misfit_b, out_map, (((2,), (1,)), ((), ())), preferred_element_type=jnp.float32)

        def retreat(later, column):
            present = cmul(conj_pair, later) + column
            return (present, present)
        adjoint, seq = lax.scan(retreat, adjoint, back.transpose(1, 0, 2), reverse=True)
        scaled = seq.transpose(1, 0, 2) * gain_pair
        adjoint_b = scaled.astype(jnp.bfloat16)
        grad_in = grad_in + lax.dot_general(adjoint_b, sig, (((0, 1), (0, 1)), ((), ())), preferred_element_type=jnp.float32)
        return ((adjoint, grad_in), scaled[:, 0])
    start_in = jnp.zeros((2 * MODES, SENSORS), jnp.float32)
    (last_adjoint, grad_in), firsts = lax.scan(backward, (start_state, start_in), (sig_blocks, misfits), reverse=True)
    out_update = grad_out / jnp.sqrt(jnp.mean(grad_out * grad_out) + 1e-06)
    in_update = grad_in / jnp.sqrt(jnp.mean(grad_in * grad_in) + 1e-06)
    boundary_adjoint = firsts.transpose(1, 0, 2)
    return (out_update, in_update, boundary_adjoint)
```

```python
import functools

import jax
import jax.numpy as jnp
from jax import lax
from jax.experimental import pallas as pl
from jax.experimental.pallas import tpu as pltpu
from jax.sharding import PartitionSpec as P

F32 = jnp.float32
BF16 = jnp.bfloat16
MESH = pl.DeviceIdType.MESH
COLS = 256


def remote(src, dst, send_sem, recv_sem, device):
    return pltpu.make_async_remote_copy(
        src_ref=src,
        dst_ref=dst,
        send_sem=send_sem,
        recv_sem=recv_sem,
        device_id={"tm": device},
        device_id_type=MESH,
    )


def cmul(ar, ai, br, bi):
    return ar * br - ai * bi, ar * bi + ai * br


class Chain:
    def __init__(self, n, pos, device_of, chunk, slots, send, recv):
        self.n, self.pos, self.device_of, self.chunk = n, pos, device_of, chunk
        self.slots, self.send, self.recv = slots, send, recv

    def turn(self, s, first):
        n, p = self.n, self.pos
        low = 2 * p < n
        right = low if first else jnp.logical_not(low)
        c = jnp.where(right, n - 1 - s, s)
        go = jnp.where(right, c > p, c < p)
        has = jnp.where(right, p > 0, p < n - 1)
        to = jnp.where(right, p + 1, p - 1)
        slot = jnp.where(right, c, jnp.where(c == p - 1, n, c))
        return c, go, has, to, slot

    def copy(self, c, slot, to):
        return remote(
            self.chunk(c), self.slots.at[slot], self.send.at[c], self.recv.at[slot], self.device_of(to)
        )

    def arrive(self, slot):
        self.copy(slot % self.n, slot, self.pos).wait_recv()

    def step(self, s):
        for first in (True, False):
            c, go, has, to, slot = self.turn(s, first)

            @pl.when(jnp.logical_and(go, has))
            def _():
                self.arrive(c)
                mine = self.chunk(c)
                mine[...] = mine[...] + self.slots[c]

            @pl.when(go)
            def _():
                self.copy(c, slot, to).start()

    def finish(self):
        n, p = self.n, self.pos
        mine = self.chunk(p)

        @pl.when(p > 0)
        def _():
            self.arrive(p)
            mine[...] = mine[...] + self.slots[p]

        @pl.when(p < n - 1)
        def _():
            self.arrive(n)
            mine[...] = mine[...] + self.slots[n]

    def drain(self):
        for c in range(self.n):

            @pl.when(self.pos != c)
            def _():
                self.copy(c, c, self.pos).wait_send()


def kernel(
    na, nb, group, rows,
    sig_ref, tgt_ref, pole_ref, gain_ref, in_hbm, out_hbm,
    upd_ref, upi_ref, bnd_ref, bnr_ref,
    inm, outm, sig_in, sig_b, work, st_b, ad_b, d_out, d_in, mis,
    e_out, e_in, f_out, f_in, sq_out, sq_in,
    gp, ys, zs, zz, zy,
    ld_sem, pair_send, pair_recv, es, er, fs, fr, qs, qr,
    ysend, yrecv, zsend, zrecv, zzsend, zzrecv, zysend, zyrecv,
):
    chips = na * nb
    n_tm = 2 * chips
    me = lax.axis_index("tm")
    core = me % 2
    chip = me // 2
    pa = chip // nb
    pb = chip % nb
    mate = chip * 2 + 1 - core
    half = pole_ref.shape[2]
    width = 2 * half
    lines = 8 * group
    n_out = outm.shape[1] // COLS

    loads = []
    for q in range(chips):
        loads.append(
            pltpu.make_async_copy(in_hbm.at[q, core], inm.at[pl.ds(q * rows, rows)], ld_sem.at[0, q])
        )
        loads.append(
            pltpu.make_async_copy(out_hbm.at[q, core], outm.at[pl.ds(q * rows, rows)], ld_sem.at[1, q])
        )
    for load in loads:
        load.start()

    barrier = pltpu.get_barrier_semaphore()

    def greet(k, _):
        other = (me + k) % n_tm
        pl.semaphore_signal(barrier, inc=1, device_id={"tm": other}, device_id_type=MESH)
        return 0

    lax.fori_loop(1, n_tm, greet, 0)
    pl.semaphore_wait(barrier, n_tm - 1)

    sig_copy = remote(sig_ref, sig_in, pair_send.at[0], pair_recv.at[0], mate)
    sig_copy.start()
    for load in loads:
        load.wait()
    sig_copy.wait()
    sig_b[...] = (sig_ref[...] + sig_in[...]).astype(BF16)

    def drive_block(i, _):
        at = pl.ds(pl.multiple_of(i * COLS, COLS), COLS)
        val = lax.dot_general(
            sig_b[...], inm[at, :], (((1,), (1,)), ((), ())), preferred_element_type=F32
        )
        work[:, :, at] = val.reshape(group, 8, COLS) * gain_ref[:, at][None]
        return 0

    lax.fori_loop(0, width // COLS, drive_block, 0)

    pr = pole_ref[0]
    pi = pole_ref[1]
    gr, gi = pr, pi
    span = 1
    while span < group:
        gr, gi = cmul(gr, gi, gr, gi)
        span *= 2
    hr, hi = cmul(gr, gi, gr, gi)
    g4r, g4i, h4r, h4i = gr[:4], gi[:4], hr[:4], hi[:4]
    zero = jnp.zeros((8, half), F32)

    def ends_step(t, carry):
        r, m = carry
        a, b = cmul(pole_ref[0], pole_ref[1], r, m)
        return a + work[t, :, :half], b + work[t, :, half:]

    er_, ei_ = lax.fori_loop(0, group, ends_step, (zero, zero), unroll=2)
    cr, ci = cmul(g4r, g4i, er_[:4], ei_[:4])
    e_out[:4, :] = cr + er_[4:]
    e_out[4:, :] = ci + ei_[4:]

    def send_fwd(q, _):
        remote(e_out, e_in.at[chip], es.at[q], er.at[chip], q * 2 + core).start()
        return 0

    lax.fori_loop(chip + 1, chips, send_fwd, 0)

    def take_fwd(q, carry):
        r, m = carry
        remote(e_out, e_in.at[q], es.at[q], er.at[q], mate).wait_recv()
        a, b = cmul(h4r, h4i, r, m)
        return a + e_in[q, :4, :], b + e_in[q, 4:, :]

    z4 = jnp.zeros((4, half), F32)
    xr, xi = lax.fori_loop(0, chip, take_fwd, (z4, z4))
    ur, ui = cmul(g4r, g4i, xr, xi)
    sr0 = jnp.concatenate([xr, ur + er_[:4]], axis=0)
    si0 = jnp.concatenate([xi, ui + ei_[:4]], axis=0)

    def state_step(k, carry):
        r, m = carry
        rs, ms = [], []
        for j in range(2):
            a, b = cmul(pole_ref[0], pole_ref[1], r, m)
            r = a + work[2 * k + j, :, :half]
            m = b + work[2 * k + j, :, half:]
            rs.append(r)
            ms.append(m)
        at = pl.ds(pl.multiple_of(k * 16, 16), 16)
        st_b[at, :half] = jnp.concatenate(rs, axis=0).astype(BF16)
        st_b[at, half:] = jnp.concatenate(ms, axis=0).astype(BF16)
        return r, m

    lax.fori_loop(0, group // 2, state_step, (sr0, si0))

    swaps = []
    for k in range(n_out):
        at = pl.ds(k * COLS, COLS)
        val = jnp.dot(st_b[...], outm[:, at], preferred_element_type=F32)
        d_out[k] = val - tgt_ref[:, at]
        swap = remote(d_out.at[k], d_in.at[k], pair_send.at[1 + k], pair_recv.at[1 + k], mate)
        swap.start()
        swaps.append(swap)

    def grad(k, left, right):
        for i in range(width // COLS):
            val = lax.dot_general(
                left[:, pl.ds(i * COLS, COLS)], right, (((0,), (0,)), ((), ())),
                preferred_element_type=F32,
            )
            if rows >= COLS:
                per = rows // COLS
                q = i // per
                gp[k, q // nb, q % nb, pl.ds((i % per) * COLS, COLS), :] = val
            else:
                for j in range(COLS // rows):
                    q = i * (COLS // rows) + j
                    gp[k, q // nb, q % nb] = val[j * rows : (j + 1) * rows]

    def a_dev(a):
        return (a * nb + pb) * 2 + core

    def b_dev(b):
        return (pa * nb + b) * 2 + core

    first_a = Chain(na, pa, a_dev, lambda c: gp.at[0, c], zz, zzsend, zzrecv)
    then_b = Chain(nb, pb, b_dev, lambda c: gp.at[0, pa, c], zy, zysend, zyrecv)
    bs = [
        Chain(nb, pb, b_dev, lambda c, k=k: gp.at[k, :, c], ys.at[k - 1], ysend.at[k - 1], yrecv.at[k - 1])
        for k in range(1, n_out + 1)
    ]
    as_ = [
        Chain(na, pa, a_dev, lambda c, k=k: gp.at[k, c, pb], zs.at[k - 1], zsend.at[k - 1], zrecv.at[k - 1])
        for k in range(1, n_out + 1)
    ]

    def run(chain, lo, hi):
        def body(s, _):
            chain.step(s)
            return 0

        lax.fori_loop(lo, hi, body, 0)

    for k in range(n_out):
        swaps[k].wait()
        mis[:, k * COLS : (k + 1) * COLS] = (d_out[k] + d_in[k]).astype(BF16)
        grad(k, st_b, mis[:, k * COLS : (k + 1) * COLS])
        if k == 0:
            first_a.step(0)
        elif k == 1:
            run(bs[0], 0, nb - 1)

    def back_block(i, _):
        at = pl.ds(pl.multiple_of(i * COLS, COLS), COLS)
        val = lax.dot_general(
            mis[...], outm[at, :], (((1,), (1,)), ((), ())), preferred_element_type=F32
        )
        work[:, :, at] = val.reshape(group, 8, COLS)
        return 0

    lax.fori_loop(0, width // COLS, back_block, 0)

    def cmulc(ar, ai, br, bi):
        return ar * br + ai * bi, ar * bi - ai * br

    def starts_step(k, carry):
        t = group - 1 - k
        r, m = carry
        a, b = cmulc(pole_ref[0], pole_ref[1], r, m)
        return a + work[t, :, :half], b + work[t, :, half:]

    br_, bi_ = lax.fori_loop(0, group, starts_step, (zero, zero), unroll=2)
    cr, ci = cmulc(g4r, g4i, br_[4:], bi_[4:])
    f_out[:4, :] = cr + br_[:4]
    f_out[4:, :] = ci + bi_[:4]

    def send_rev(q, _):
        remote(f_out, f_in.at[chip], fs.at[q], fr.at[chip], q * 2 + core).start()
        return 0

    lax.fori_loop(0, chip, send_rev, 0)

    def take_rev(k, carry):
        q = chips - 1 - k
        r, m = carry
        remote(f_out, f_in.at[q], fs.at[q], fr.at[q], mate).wait_recv()
        a, b = cmulc(h4r, h4i, r, m)
        return a + f_in[q, :4, :], b + f_in[q, 4:, :]

    xr, xi = lax.fori_loop(0, chips - 1 - chip, take_rev, (z4, z4))
    ur, ui = cmulc(g4r, g4i, xr, xi)
    ar0 = jnp.concatenate([ur + br_[4:], xr], axis=0)
    ai0 = jnp.concatenate([ui + bi_[4:], xi], axis=0)

    def adj_step(k, carry):
        r, m = carry
        k2 = group // 2 - 1 - k
        rs, ms = [], []
        for j in (1, 0):
            a, b = cmulc(pole_ref[0], pole_ref[1], r, m)
            r = a + work[2 * k2 + j, :, :half]
            m = b + work[2 * k2 + j, :, half:]
            rs.insert(0, r * gain_ref[:, :half])
            ms.insert(0, m * gain_ref[:, half:])
        at = pl.ds(pl.multiple_of(k2 * 16, 16), 16)
        ad_b[at, :half] = jnp.concatenate(rs, axis=0).astype(BF16)
        ad_b[at, half:] = jnp.concatenate(ms, axis=0).astype(BF16)
        return r, m

    ar_, ai_ = lax.fori_loop(0, group // 2, adj_step, (ar0, ai0))
    bnd_ref[:, :half] = ar_ * gain_ref[:, :half]
    bnd_ref[:, half:] = ai_ * gain_ref[:, half:]
    bnd_copy = remote(
        bnd_ref, bnr_ref, pair_send.at[1 + n_out], pair_recv.at[1 + n_out], mate
    )
    bnd_copy.start()

    grad(n_out, ad_b, sig_b[...])

    run(first_a, 1, na - 1)
    for k in range(n_out):
        bs[k].finish()
        if k + 1 < n_out:
            run(bs[k + 1], 0, nb - 1)
        if k == 0:
            first_a.finish()
            run(then_b, 0, nb - 1)
            run(as_[0], 0, na - 1)
        else:
            run(as_[k], 0, na - 1)
            as_[k - 1].finish()
    then_b.finish()
    as_[n_out - 1].finish()

    def part(x):
        v = jnp.sum((x * x).reshape(rows // 8, 8, COLS), axis=0)
        return v[:, :128] + v[:, 128:]

    total = part(gp[0, pa, pb])
    for k in range(1, n_out):
        total = total + part(gp[k, pa, pb])
    sq_out[0] = total
    sq_out[1] = part(gp[n_out, pa, pb])

    def send_sq(k, _):
        other = (me + k) % n_tm
        remote(sq_out, sq_in.at[me], qs.at[other], qr.at[me], other).start()
        return 0

    lax.fori_loop(1, n_tm, send_sq, 0)
    sq_in[me] = sq_out[...]

    def take_sq(k, _):
        other = (me + k) % n_tm
        remote(sq_out, sq_in.at[other], qs.at[other], qr.at[other], other).wait_recv()
        return 0

    lax.fori_loop(1, n_tm, take_sq, 0)
    sums = jnp.sum(sq_in[...], axis=0)
    count = 2.0 * width
    out_scale = lax.rsqrt(jnp.sum(sums[0], keepdims=True) / (count * COLS * n_out) + 1e-6)
    in_scale = lax.rsqrt(jnp.sum(sums[1], keepdims=True) / (count * COLS) + 1e-6)
    for k in range(n_out):
        upd_ref[:, k * COLS : (k + 1) * COLS] = gp[k, pa, pb] * out_scale
    upi_ref[...] = gp[n_out, pa, pb] * in_scale

    def sent_sq(k, _):
        other = (me + k) % n_tm
        remote(sq_out, sq_in.at[me], qs.at[other], qr.at[me], other).wait_send()
        return 0

    lax.fori_loop(1, n_tm, sent_sq, 0)

    def sent_fwd(q, _):
        remote(e_out, e_in.at[chip], es.at[q], er.at[chip], q * 2 + core).wait_send()
        return 0

    lax.fori_loop(chip + 1, chips, sent_fwd, 0)

    def sent_rev(q, _):
        remote(f_out, f_in.at[chip], fs.at[q], fr.at[chip], q * 2 + core).wait_send()
        return 0

    lax.fori_loop(0, chip, sent_rev, 0)
    bnd_copy.wait()
    for chain in [first_a, then_b] + bs + as_:
        chain.drain()


def per_device(na, nb, signals, targets, decay_rate, pole_angle, in_map, out_map):
    members, group, sensors = signals.shape
    modes = decay_rate.shape[0]
    chips = na * nb
    rows = in_map.shape[0] // (2 * chips)
    core = lax.axis_index("tm") % 2
    half = modes // 2
    width = modes
    n_out = out_map.shape[1] // COLS
    lines = 2 * members * group

    def padded(x):
        x = jnp.transpose(x, (1, 0, 2)).astype(F32)
        low = jnp.where(core == 0, x, 0.0)
        high = jnp.where(core == 0, 0.0, x)
        return jnp.concatenate([low, high], axis=1).reshape(lines, x.shape[2])

    def own(x):
        return lax.dynamic_index_in_dim(x.reshape(-1, 2, rows), core, 1, False).reshape(half)

    rate, angle = own(decay_rate), own(pole_angle)
    size = jnp.exp(-rate)
    pole = jnp.stack([size * jnp.cos(angle), size * jnp.sin(angle)])
    pole = jnp.broadcast_to(pole[:, None, :], (2, 8, half))
    gain = jnp.sqrt(-jnp.expm1(-2.0 * rate))
    gain = jnp.broadcast_to(jnp.concatenate([gain, gain])[None], (8, width))

    vm = pl.BlockSpec(memory_space=pltpu.VMEM)
    anyw = pl.BlockSpec(memory_space=pl.ANY)
    dma = pltpu.SemaphoreType.DMA
    scratch = [
        pltpu.VMEM((width, sensors), BF16),
        pltpu.VMEM((width, n_out * COLS), BF16),
        pltpu.VMEM((lines, sensors), F32),
        pltpu.VMEM((lines, sensors), BF16),
        pltpu.VMEM((group, 8, width), F32),
        pltpu.VMEM((lines, width), BF16),
        pltpu.VMEM((lines, width), BF16),
        pltpu.VMEM((n_out, lines, COLS), F32),
        pltpu.VMEM((n_out, lines, COLS), F32),
        pltpu.VMEM((lines, n_out * COLS), BF16),
        pltpu.VMEM((8, half), F32),
        pltpu.VMEM((chips, 8, half), F32),
        pltpu.VMEM((8, half), F32),
        pltpu.VMEM((chips, 8, half), F32),
        pltpu.VMEM((2, 8, 128), F32),
        pltpu.VMEM((2 * chips, 2, 8, 128), F32),
        pltpu.VMEM((n_out + 1, na, nb, rows, COLS), F32),
        pltpu.VMEM((n_out, nb + 1, na, rows, COLS), F32),
        pltpu.VMEM((n_out, na + 1, rows, COLS), F32),
        pltpu.VMEM((na + 1, nb, rows, COLS), F32),
        pltpu.VMEM((nb + 1, rows, COLS), F32),
        dma((2, chips)),
        dma((n_out + 2,)),
        dma((n_out + 2,)),
        dma((chips,)),
        dma((chips,)),
        dma((chips,)),
        dma((chips,)),
        dma((2 * chips,)),
        dma((2 * chips,)),
        dma((n_out, nb)),
        dma((n_out, nb + 1)),
        dma((n_out, na)),
        dma((n_out, na + 1)),
        dma((na,)),
        dma((na + 1,)),
        dma((nb,)),
        dma((nb + 1,)),
    ]
    upd, upi, bnd, bnr = pl.pallas_call(
        functools.partial(kernel, na, nb, group, rows),
        out_shape=(
            jax.ShapeDtypeStruct((rows, n_out * COLS), F32),
            jax.ShapeDtypeStruct((rows, sensors), F32),
            jax.ShapeDtypeStruct((8, width), F32),
            jax.ShapeDtypeStruct((8, width), F32),
        ),
        in_specs=[vm, vm, vm, vm, anyw, anyw],
        out_specs=(vm, vm, vm, vm),
        scratch_shapes=scratch,
        compiler_params=pltpu.CompilerParams(
            collective_id=0, has_side_effects=True, vmem_limit_bytes=62 * 1024 * 1024
        ),
    )(
        padded(signals),
        padded(targets),
        pole,
        gain,
        in_map.reshape(chips, 2, rows, sensors),
        out_map.reshape(chips, 2, rows, n_out * COLS),
    )
    bnd = lax.dynamic_slice_in_dim(bnd, core * members, members, 0).reshape(members, chips, rows)
    bnr = lax.dynamic_slice_in_dim(bnr, core * members, members, 0).reshape(members, chips, rows)
    even = jnp.where(core == 0, bnd, bnr)
    odd = jnp.where(core == 0, bnr, bnd)
    boundary = jnp.stack([even, odd], axis=2).reshape(members, 1, 2 * width)
    return upd, upi, boundary


def solution(mesh):
    chips = mesh.shape["tm"] // 2
    nb = 1
    while 4 * nb * nb <= chips:
        nb *= 2
    na = chips // nb
    return jax.shard_map(
        functools.partial(per_device, na, nb),
        mesh=mesh,
        in_specs=(
            P("grp", "tm", None),
            P("grp", "tm", None),
            P("grp"),
            P("grp"),
            P("grp", None),
            P("grp", None),
        ),
        out_specs=(P(("grp", "tm"), None), P(("grp", "tm"), None), P("grp", "tm", None)),
        check_vma=False,
    )
```

```python
import functools

import jax
import jax.numpy as jnp
from jax import lax
from jax.experimental import pallas as pl
from jax.experimental.pallas import tpu as pltpu
from jax.sharding import PartitionSpec as P

F32 = jnp.float32
BF16 = jnp.bfloat16
MESH = pl.DeviceIdType.MESH
COLS = 256


def remote(src, dst, send_sem, recv_sem, device):
    return pltpu.make_async_remote_copy(
        src_ref=src,
        dst_ref=dst,
        send_sem=send_sem,
        recv_sem=recv_sem,
        device_id={"tm": device},
        device_id_type=MESH,
    )


def cmul(ar, ai, br, bi):
    return ar * br - ai * bi, ar * bi + ai * br


class Chain:
    def __init__(self, n, pos, device_of, chunk, slots, send, recv):
        self.n, self.pos, self.device_of, self.chunk = n, pos, device_of, chunk
        self.slots, self.send, self.recv = slots, send, recv

    def copy(self, c, slot, to):
        return remote(
            self.chunk(c), self.slots.at[slot], self.send.at[c], self.recv.at[slot], self.device_of(to)
        )

    def arrive(self, slot):
        self.copy(slot % self.n, slot, self.pos).wait_recv()

    def launch(self, c, right):
        to = jnp.where(right, self.pos + 1, self.pos - 1)
        slot = jnp.where(jnp.logical_and(jnp.logical_not(right), c == self.pos - 1), self.n, c)
        self.copy(c, slot, to).start()

    def lead(self):
        n, p = self.n, self.pos

        @pl.when(jnp.logical_or(p == 0, p == n - 1))
        def _():
            def body(s, _):
                right = p == 0
                self.launch(jnp.where(right, n - 1 - s, s), right)
                return 0

            lax.fori_loop(0, n - 1, body, 0)

    def pass_on(self, s, first):
        n, p = self.n, self.pos
        low = 2 * p < n
        right = low if first else jnp.logical_not(low)
        c = jnp.where(right, n - 1 - s, s)
        go = jnp.where(right, jnp.logical_and(c > p, p > 0), jnp.logical_and(c < p, p < n - 1))

        @pl.when(go)
        def _():
            self.arrive(c)
            mine = self.chunk(c)
            mine[...] = mine[...] + self.slots[c]
            self.launch(c, right)

    def step(self, s):
        if self.n > 2:
            self.pass_on(s, True)
            self.pass_on(s, False)

    def finish(self):
        n, p = self.n, self.pos
        mine = self.chunk(p)

        @pl.when(p > 0)
        def _():
            self.arrive(p)
            mine[...] = mine[...] + self.slots[p]

        @pl.when(p < n - 1)
        def _():
            self.arrive(n)
            mine[...] = mine[...] + self.slots[n]

    def drain(self):
        for c in range(self.n):

            @pl.when(self.pos != c)
            def _():
                self.copy(c, c, self.pos).wait_send()


def kernel(
    na, nb, group, rows,
    sig_ref, tgt_ref, pole_ref, gain_ref, in_hbm, out_hbm,
    upd_ref, upi_ref, bnd_ref, bnr_ref,
    inm, outm, sig_in, sig_b, work, st_b, ad_b, d_out, d_in, mis,
    e_out, e_in, f_out, f_in, sq_out, sq_in,
    gp, ys, zs, zz, zy,
    ld_sem, pair_send, pair_recv, es, er, fs, fr, qs, qr,
    ysend, yrecv, zsend, zrecv, zzsend, zzrecv, zysend, zyrecv,
):
    chips = na * nb
    n_tm = 2 * chips
    me = lax.axis_index("tm")
    core = me % 2
    chip = me // 2
    pa = chip // nb
    pb = chip % nb
    mate = chip * 2 + 1 - core
    half = pole_ref.shape[2]
    width = 2 * half
    lines = 8 * group
    n_out = outm.shape[1] // COLS

    loads = []
    for q in range(chips):
        loads.append(
            pltpu.make_async_copy(in_hbm.at[q, core], inm.at[pl.ds(q * rows, rows)], ld_sem.at[0, q])
        )
        loads.append(
            pltpu.make_async_copy(out_hbm.at[q, core], outm.at[pl.ds(q * rows, rows)], ld_sem.at[1, q])
        )
    for load in loads:
        load.start()

    barrier = pltpu.get_barrier_semaphore()

    def greet(k, _):
        other = (me + k) % n_tm
        pl.semaphore_signal(barrier, inc=1, device_id={"tm": other}, device_id_type=MESH)
        return 0

    lax.fori_loop(1, n_tm, greet, 0)
    pl.semaphore_wait(barrier, n_tm - 1)

    sig_copy = remote(sig_ref, sig_in, pair_send.at[0], pair_recv.at[0], mate)
    sig_copy.start()
    for load in loads:
        load.wait()
    sig_copy.wait()
    sig_b[...] = (sig_ref[...] + sig_in[...]).astype(BF16)

    def drive_block(i, _):
        at = pl.ds(pl.multiple_of(i * COLS, COLS), COLS)
        val = lax.dot_general(
            sig_b[...], inm[at, :], (((1,), (1,)), ((), ())), preferred_element_type=F32
        )
        work[:, :, at] = val.reshape(group, 8, COLS) * gain_ref[:, at][None]
        return 0

    lax.fori_loop(0, width // COLS, drive_block, 0)

    pr = pole_ref[0]
    pi = pole_ref[1]
    gr, gi = pr, pi
    span = 1
    while span < group:
        gr, gi = cmul(gr, gi, gr, gi)
        span *= 2
    hr, hi = cmul(gr, gi, gr, gi)
    g4r, g4i, h4r, h4i = gr[:4], gi[:4], hr[:4], hi[:4]
    zero = jnp.zeros((8, half), F32)

    def ends_step(t, carry):
        r, m = carry
        a, b = cmul(pole_ref[0], pole_ref[1], r, m)
        return a + work[t, :, :half], b + work[t, :, half:]

    er_, ei_ = lax.fori_loop(0, group, ends_step, (zero, zero), unroll=2)
    cr, ci = cmul(g4r, g4i, er_[:4], ei_[:4])
    e_out[:4, :] = cr + er_[4:]
    e_out[4:, :] = ci + ei_[4:]

    def send_fwd(q, _):
        remote(e_out, e_in.at[chip], es.at[q], er.at[chip], q * 2 + core).start()
        return 0

    lax.fori_loop(chip + 1, chips, send_fwd, 0)

    def take_fwd(q, carry):
        r, m = carry
        remote(e_out, e_in.at[q], es.at[q], er.at[q], mate).wait_recv()
        a, b = cmul(h4r, h4i, r, m)
        return a + e_in[q, :4, :], b + e_in[q, 4:, :]

    z4 = jnp.zeros((4, half), F32)
    xr, xi = lax.fori_loop(0, chip, take_fwd, (z4, z4))
    ur, ui = cmul(g4r, g4i, xr, xi)
    sr0 = jnp.concatenate([xr, ur + er_[:4]], axis=0)
    si0 = jnp.concatenate([xi, ui + ei_[:4]], axis=0)

    def state_step(k, carry):
        r, m = carry
        rs, ms = [], []
        for j in range(2):
            a, b = cmul(pole_ref[0], pole_ref[1], r, m)
            r = a + work[2 * k + j, :, :half]
            m = b + work[2 * k + j, :, half:]
            rs.append(r)
            ms.append(m)
        at = pl.ds(pl.multiple_of(k * 16, 16), 16)
        st_b[at, :half] = jnp.concatenate(rs, axis=0).astype(BF16)
        st_b[at, half:] = jnp.concatenate(ms, axis=0).astype(BF16)
        return r, m

    lax.fori_loop(0, group // 2, state_step, (sr0, si0))

    swaps = []
    for k in range(n_out):
        at = pl.ds(k * COLS, COLS)
        val = jnp.dot(st_b[...], outm[:, at], preferred_element_type=F32)
        d_out[k] = val - tgt_ref[:, at]
        swap = remote(d_out.at[k], d_in.at[k], pair_send.at[1 + k], pair_recv.at[1 + k], mate)
        swap.start()
        swaps.append(swap)

    def grad(k, left, right):
        for i in range(width // COLS):
            val = lax.dot_general(
                left[:, pl.ds(i * COLS, COLS)], right, (((0,), (0,)), ((), ())),
                preferred_element_type=F32,
            )
            if rows >= COLS:
                per = rows // COLS
                q = i // per
                gp[k, q // nb, q % nb, pl.ds((i % per) * COLS, COLS), :] = val
            else:
                for j in range(COLS // rows):
                    q = i * (COLS // rows) + j
                    gp[k, q // nb, q % nb] = val[j * rows : (j + 1) * rows]

    def a_dev(a):
        return (a * nb + pb) * 2 + core

    def b_dev(b):
        return (pa * nb + b) * 2 + core

    first_a = Chain(na, pa, a_dev, lambda c: gp.at[0, c], zz, zzsend, zzrecv)
    then_b = Chain(nb, pb, b_dev, lambda c: gp.at[0, pa, c], zy, zysend, zyrecv)
    bs = [
        Chain(nb, pb, b_dev, lambda c, k=k: gp.at[k, :, c], ys.at[k - 1], ysend.at[k - 1], yrecv.at[k - 1])
        for k in range(1, n_out + 1)
    ]
    as_ = [
        Chain(na, pa, a_dev, lambda c, k=k: gp.at[k, c, pb], zs.at[k - 1], zsend.at[k - 1], zrecv.at[k - 1])
        for k in range(1, n_out + 1)
    ]

    def run(chain, lo, hi):
        if chain.n > 2:

            def body(s, _):
                chain.step(s)
                return 0

            lax.fori_loop(lo, hi, body, 0)

    for k in range(n_out):
        swaps[k].wait()
        mis[:, k * COLS : (k + 1) * COLS] = (d_out[k] + d_in[k]).astype(BF16)
        grad(k, st_b, mis[:, k * COLS : (k + 1) * COLS])
        if k == 0:
            first_a.lead()
        else:
            bs[k - 1].lead()

    def back_block(i, _):
        at = pl.ds(pl.multiple_of(i * COLS, COLS), COLS)
        val = lax.dot_general(
            mis[...], outm[at, :], (((1,), (1,)), ((), ())), preferred_element_type=F32
        )
        work[:, :, at] = val.reshape(group, 8, COLS)
        return 0

    lax.fori_loop(0, width // COLS, back_block, 0)

    def cmulc(ar, ai, br, bi):
        return ar * br + ai * bi, ar * bi - ai * br

    def starts_step(k, carry):
        t = group - 1 - k
        r, m = carry
        a, b = cmulc(pole_ref[0], pole_ref[1], r, m)
        return a + work[t, :, :half], b + work[t, :, half:]

    br_, bi_ = lax.fori_loop(0, group, starts_step, (zero, zero), unroll=2)
    cr, ci = cmulc(g4r, g4i, br_[4:], bi_[4:])
    f_out[:4, :] = cr + br_[:4]
    f_out[4:, :] = ci + bi_[:4]

    def send_rev(q, _):
        remote(f_out, f_in.at[chip], fs.at[q], fr.at[chip], q * 2 + core).start()
        return 0

    lax.fori_loop(0, chip, send_rev, 0)
    first_a.pass_on(0, True)

    def take_rev(k, carry):
        q = chips - 1 - k
        r, m = carry
        remote(f_out, f_in.at[q], fs.at[q], fr.at[q], mate).wait_recv()
        a, b = cmulc(h4r, h4i, r, m)
        return a + f_in[q, :4, :], b + f_in[q, 4:, :]

    xr, xi = lax.fori_loop(0, chips - 1 - chip, take_rev, (z4, z4))
    ur, ui = cmulc(g4r, g4i, xr, xi)
    ar0 = jnp.concatenate([ur + br_[4:], xr], axis=0)
    ai0 = jnp.concatenate([ui + bi_[4:], xi], axis=0)

    def adj_step(k, carry):
        r, m = carry
        k2 = group // 2 - 1 - k
        rs, ms = [], []
        for j in (1, 0):
            a, b = cmulc(pole_ref[0], pole_ref[1], r, m)
            r = a + work[2 * k2 + j, :, :half]
            m = b + work[2 * k2 + j, :, half:]
            rs.insert(0, r * gain_ref[:, :half])
            ms.insert(0, m * gain_ref[:, half:])
        at = pl.ds(pl.multiple_of(k2 * 16, 16), 16)
        ad_b[at, :half] = jnp.concatenate(rs, axis=0).astype(BF16)
        ad_b[at, half:] = jnp.concatenate(ms, axis=0).astype(BF16)
        return r, m

    ar_, ai_ = lax.fori_loop(0, group // 2, adj_step, (ar0, ai0))
    bnd_ref[:, :half] = ar_ * gain_ref[:, :half]
    bnd_ref[:, half:] = ai_ * gain_ref[:, half:]
    bnd_copy = remote(
        bnd_ref, bnr_ref, pair_send.at[1 + n_out], pair_recv.at[1 + n_out], mate
    )
    bnd_copy.start()

    grad(n_out, ad_b, sig_b[...])

    bs[n_out - 1].lead()
    first_a.pass_on(0, False)
    for k in range(n_out):
        if k == 0:
            run(first_a, 1, na - 1)
        run(bs[k], 0, nb - 1)
        bs[k].finish()
        as_[k].lead()
        if k == 0:
            first_a.finish()
            then_b.lead()
        else:
            as_[k - 1].finish()
        run(as_[k], 0, na - 1)
    run(then_b, 0, nb - 1)
    then_b.finish()
    as_[n_out - 1].finish()

    def part(x):
        v = jnp.sum((x * x).reshape(rows // 8, 8, COLS), axis=0)
        return v[:, :128] + v[:, 128:]

    total = part(gp[0, pa, pb])
    for k in range(1, n_out):
        total = total + part(gp[k, pa, pb])
    sq_out[0] = total
    sq_out[1] = part(gp[n_out, pa, pb])

    def send_sq(k, _):
        other = (me + k) % n_tm
        remote(sq_out, sq_in.at[me], qs.at[other], qr.at[me], other).start()
        return 0

    lax.fori_loop(1, n_tm, send_sq, 0)
    sq_in[me] = sq_out[...]

    def take_sq(k, _):
        other = (me + k) % n_tm
        remote(sq_out, sq_in.at[other], qs.at[other], qr.at[other], other).wait_recv()
        return 0

    lax.fori_loop(1, n_tm, take_sq, 0)
    sums = jnp.sum(sq_in[...], axis=0)
    count = 2.0 * width
    out_scale = lax.rsqrt(jnp.sum(sums[0], keepdims=True) / (count * COLS * n_out) + 1e-6)
    in_scale = lax.rsqrt(jnp.sum(sums[1], keepdims=True) / (count * COLS) + 1e-6)
    for k in range(n_out):
        upd_ref[:, k * COLS : (k + 1) * COLS] = gp[k, pa, pb] * out_scale
    upi_ref[...] = gp[n_out, pa, pb] * in_scale

    def sent_sq(k, _):
        other = (me + k) % n_tm
        remote(sq_out, sq_in.at[me], qs.at[other], qr.at[me], other).wait_send()
        return 0

    lax.fori_loop(1, n_tm, sent_sq, 0)

    def sent_fwd(q, _):
        remote(e_out, e_in.at[chip], es.at[q], er.at[chip], q * 2 + core).wait_send()
        return 0

    lax.fori_loop(chip + 1, chips, sent_fwd, 0)

    def sent_rev(q, _):
        remote(f_out, f_in.at[chip], fs.at[q], fr.at[chip], q * 2 + core).wait_send()
        return 0

    lax.fori_loop(0, chip, sent_rev, 0)
    bnd_copy.wait()
    for chain in [first_a, then_b] + bs + as_:
        chain.drain()


def per_device(na, nb, signals, targets, decay_rate, pole_angle, in_map, out_map):
    members, group, sensors = signals.shape
    modes = decay_rate.shape[0]
    chips = na * nb
    rows = in_map.shape[0] // (2 * chips)
    core = lax.axis_index("tm") % 2
    half = modes // 2
    width = modes
    n_out = out_map.shape[1] // COLS
    lines = 2 * members * group

    def padded(x):
        x = jnp.transpose(x, (1, 0, 2)).astype(F32)
        low = jnp.where(core == 0, x, 0.0)
        high = jnp.where(core == 0, 0.0, x)
        return jnp.concatenate([low, high], axis=1).reshape(lines, x.shape[2])

    def own(x):
        return lax.dynamic_index_in_dim(x.reshape(-1, 2, rows), core, 1, False).reshape(half)

    rate, angle = own(decay_rate), own(pole_angle)
    size = jnp.exp(-rate)
    pole = jnp.stack([size * jnp.cos(angle), size * jnp.sin(angle)])
    pole = jnp.broadcast_to(pole[:, None, :], (2, 8, half))
    gain = jnp.sqrt(-jnp.expm1(-2.0 * rate))
    gain = jnp.broadcast_to(jnp.concatenate([gain, gain])[None], (8, width))

    vm = pl.BlockSpec(memory_space=pltpu.VMEM)
    anyw = pl.BlockSpec(memory_space=pl.ANY)
    dma = pltpu.SemaphoreType.DMA
    scratch = [
        pltpu.VMEM((width, sensors), BF16),
        pltpu.VMEM((width, n_out * COLS), BF16),
        pltpu.VMEM((lines, sensors), F32),
        pltpu.VMEM((lines, sensors), BF16),
        pltpu.VMEM((group, 8, width), F32),
        pltpu.VMEM((lines, width), BF16),
        pltpu.VMEM((lines, width), BF16),
        pltpu.VMEM((n_out, lines, COLS), F32),
        pltpu.VMEM((n_out, lines, COLS), F32),
        pltpu.VMEM((lines, n_out * COLS), BF16),
        pltpu.VMEM((8, half), F32),
        pltpu.VMEM((chips, 8, half), F32),
        pltpu.VMEM((8, half), F32),
        pltpu.VMEM((chips, 8, half), F32),
        pltpu.VMEM((2, 8, 128), F32),
        pltpu.VMEM((2 * chips, 2, 8, 128), F32),
        pltpu.VMEM((n_out + 1, na, nb, rows, COLS), F32),
        pltpu.VMEM((n_out, nb + 1, na, rows, COLS), F32),
        pltpu.VMEM((n_out, na + 1, rows, COLS), F32),
        pltpu.VMEM((na + 1, nb, rows, COLS), F32),
        pltpu.VMEM((nb + 1, rows, COLS), F32),
        dma((2, chips)),
        dma((n_out + 2,)),
        dma((n_out + 2,)),
        dma((chips,)),
        dma((chips,)),
        dma((chips,)),
        dma((chips,)),
        dma((2 * chips,)),
        dma((2 * chips,)),
        dma((n_out, nb)),
        dma((n_out, nb + 1)),
        dma((n_out, na)),
        dma((n_out, na + 1)),
        dma((na,)),
        dma((na + 1,)),
        dma((nb,)),
        dma((nb + 1,)),
    ]
    upd, upi, bnd, bnr = pl.pallas_call(
        functools.partial(kernel, na, nb, group, rows),
        out_shape=(
            jax.ShapeDtypeStruct((rows, n_out * COLS), F32),
            jax.ShapeDtypeStruct((rows, sensors), F32),
            jax.ShapeDtypeStruct((8, width), F32),
            jax.ShapeDtypeStruct((8, width), F32),
        ),
        in_specs=[vm, vm, vm, vm, anyw, anyw],
        out_specs=(vm, vm, vm, vm),
        scratch_shapes=scratch,
        compiler_params=pltpu.CompilerParams(
            collective_id=0, has_side_effects=True, vmem_limit_bytes=62 * 1024 * 1024
        ),
    )(
        padded(signals),
        padded(targets),
        pole,
        gain,
        in_map.reshape(chips, 2, rows, sensors),
        out_map.reshape(chips, 2, rows, n_out * COLS),
    )
    bnd = lax.dynamic_slice_in_dim(bnd, core * members, members, 0).reshape(members, chips, rows)
    bnr = lax.dynamic_slice_in_dim(bnr, core * members, members, 0).reshape(members, chips, rows)
    even = jnp.where(core == 0, bnd, bnr)
    odd = jnp.where(core == 0, bnr, bnd)
    boundary = jnp.stack([even, odd], axis=2).reshape(members, 1, 2 * width)
    return upd, upi, boundary


def solution(mesh):
    chips = mesh.shape["tm"] // 2
    nb = 1
    while 4 * nb * nb <= chips:
        nb *= 2
    na = chips // nb
    return jax.shard_map(
        functools.partial(per_device, na, nb),
        mesh=mesh,
        in_specs=(
            P("grp", "tm", None),
            P("grp", "tm", None),
            P("grp"),
            P("grp"),
            P("grp", None),
            P("grp", None),
        ),
        out_specs=(P(("grp", "tm"), None), P(("grp", "tm"), None), P("grp", "tm", None)),
        check_vma=False,
    )
```

```python
import functools

import jax
import jax.numpy as jnp
from jax import lax
from jax.experimental import pallas as pl
from jax.experimental.pallas import tpu as pltpu
from jax.sharding import PartitionSpec as P

F32 = jnp.float32
BF16 = jnp.bfloat16
MESH = pl.DeviceIdType.MESH
COLS = 256


def remote(src, dst, send_sem, recv_sem, device):
    return pltpu.make_async_remote_copy(
        src_ref=src,
        dst_ref=dst,
        send_sem=send_sem,
        recv_sem=recv_sem,
        device_id={"tm": device},
        device_id_type=MESH,
    )


def cmul(ar, ai, br, bi):
    return ar * br - ai * bi, ar * bi + ai * br


class Chain:
    def __init__(self, n, pos, device_of, chunk, slots, send, recv):
        self.n, self.pos, self.device_of, self.chunk = n, pos, device_of, chunk
        self.slots, self.send, self.recv = slots, send, recv

    def copy(self, c, slot, to):
        return remote(
            self.chunk(c), self.slots.at[slot], self.send.at[c], self.recv.at[slot], self.device_of(to)
        )

    def arrive(self, slot):
        self.copy(slot % self.n, slot, self.pos).wait_recv()

    def launch(self, c, right):
        to = jnp.where(right, self.pos + 1, self.pos - 1)
        slot = jnp.where(jnp.logical_and(jnp.logical_not(right), c == self.pos - 1), self.n, c)
        self.copy(c, slot, to).start()

    def lead(self):
        n, p = self.n, self.pos

        @pl.when(jnp.logical_or(p == 0, p == n - 1))
        def _():
            def body(s, _):
                right = p == 0
                self.launch(jnp.where(right, n - 1 - s, s), right)
                return 0

            lax.fori_loop(0, n - 1, body, 0)

    def pass_on(self, s, first):
        n, p = self.n, self.pos
        low = 2 * p < n
        right = low if first else jnp.logical_not(low)
        c = jnp.where(right, n - 1 - s, s)
        go = jnp.where(right, jnp.logical_and(c > p, p > 0), jnp.logical_and(c < p, p < n - 1))

        @pl.when(go)
        def _():
            self.arrive(c)
            mine = self.chunk(c)
            mine[...] = mine[...] + self.slots[c]
            self.launch(c, right)

    def step(self, s):
        if self.n > 2:
            self.pass_on(s, True)
            self.pass_on(s, False)

    def finish(self):
        n, p = self.n, self.pos
        mine = self.chunk(p)

        @pl.when(p > 0)
        def _():
            self.arrive(p)
            mine[...] = mine[...] + self.slots[p]

        @pl.when(p < n - 1)
        def _():
            self.arrive(n)
            mine[...] = mine[...] + self.slots[n]

    def drain(self):
        for c in range(self.n):

            @pl.when(self.pos != c)
            def _():
                self.copy(c, c, self.pos).wait_send()


def kernel(
    na, nb, group, rows,
    sig_ref, tgt_ref, pole_row, gain_ref, in_hbm, out_hbm,
    upd_ref, upi_ref, bnd_ref, bnr_ref,
    inm, outm, sig_in, sig_b, work, st_b, ad_b, d_out, d_in, mis,
    e_out, e_in, f_out, f_in, sq_out, sq_in,
    gp, ys, zs, zz, zy, sig8, tgt8, pole_ref,
    ld_sem, pair_send, pair_recv, es, er, fs, fr, qs, qr,
    ysend, yrecv, zsend, zrecv, zzsend, zzrecv, zysend, zyrecv,
):
    chips = na * nb
    n_tm = 2 * chips
    me = lax.axis_index("tm")
    core = me % 2
    chip = me // 2
    pa = chip // nb
    pb = chip % nb
    mate = chip * 2 + 1 - core
    half = pole_row.shape[2]
    width = 2 * half
    lines = 8 * group
    n_out = outm.shape[1] // COLS

    loads = []
    for q in range(chips):
        loads.append(
            pltpu.make_async_copy(in_hbm.at[q, core], inm.at[pl.ds(q * rows, rows)], ld_sem.at[0, q])
        )
        loads.append(
            pltpu.make_async_copy(out_hbm.at[q, core], outm.at[pl.ds(q * rows, rows)], ld_sem.at[1, q])
        )
    for load in loads:
        load.start()

    def interleave(wide, x_ref):
        wide[...] = jnp.zeros(wide.shape, F32)
        for c in range(2):

            @pl.when(core == c)
            def _():
                for m in range(4):
                    wide[:, 4 * c + m, :] = x_ref[m].astype(F32)

    interleave(sig8, sig_ref)
    pole_ref[...] = jnp.broadcast_to(pole_row[...], pole_ref.shape)

    barrier = pltpu.get_barrier_semaphore()

    def greet(k, _):
        other = (me + k) % n_tm
        pl.semaphore_signal(barrier, inc=1, device_id={"tm": other}, device_id_type=MESH)
        return 0

    lax.fori_loop(1, n_tm, greet, 0)
    pl.semaphore_wait(barrier, n_tm - 1)

    sig_copy = remote(sig8, sig_in, pair_send.at[0], pair_recv.at[0], mate)
    sig_copy.start()
    for load in loads:
        load.wait()
    sig_copy.wait()
    sig_b[...] = (sig8[...] + sig_in[...]).reshape(sig_b.shape).astype(BF16)

    def drive_block(i, _):
        at = pl.ds(pl.multiple_of(i * COLS, COLS), COLS)
        val = lax.dot_general(
            sig_b[...], inm[at, :], (((1,), (1,)), ((), ())), preferred_element_type=F32
        )
        work[:, :, at] = val.reshape(group, 8, COLS) * gain_ref[:, at][None]
        return 0

    lax.fori_loop(0, width // COLS, drive_block, 0)

    pr = pole_ref[0]
    pi = pole_ref[1]
    gr, gi = pr, pi
    span = 1
    while span < group:
        gr, gi = cmul(gr, gi, gr, gi)
        span *= 2
    hr, hi = cmul(gr, gi, gr, gi)
    g4r, g4i, h4r, h4i = gr[:4], gi[:4], hr[:4], hi[:4]
    zero = jnp.zeros((8, half), F32)

    def ends_step(t, carry):
        r, m = carry
        a, b = cmul(pole_ref[0], pole_ref[1], r, m)
        return a + work[t, :, :half], b + work[t, :, half:]

    er_, ei_ = lax.fori_loop(0, group, ends_step, (zero, zero), unroll=2)
    cr, ci = cmul(g4r, g4i, er_[:4], ei_[:4])
    e_out[:4, :] = cr + er_[4:]
    e_out[4:, :] = ci + ei_[4:]

    def send_fwd(q, _):
        remote(e_out, e_in.at[chip], es.at[q], er.at[chip], q * 2 + core).start()
        return 0

    lax.fori_loop(chip + 1, chips, send_fwd, 0)
    interleave(tgt8, tgt_ref)

    def take_fwd(q, carry):
        r, m = carry
        remote(e_out, e_in.at[q], es.at[q], er.at[q], mate).wait_recv()
        a, b = cmul(h4r, h4i, r, m)
        return a + e_in[q, :4, :], b + e_in[q, 4:, :]

    z4 = jnp.zeros((4, half), F32)
    xr, xi = lax.fori_loop(0, chip, take_fwd, (z4, z4))
    ur, ui = cmul(g4r, g4i, xr, xi)
    sr0 = jnp.concatenate([xr, ur + er_[:4]], axis=0)
    si0 = jnp.concatenate([xi, ui + ei_[:4]], axis=0)

    def state_step(k, carry):
        r, m = carry
        rs, ms = [], []
        for j in range(2):
            a, b = cmul(pole_ref[0], pole_ref[1], r, m)
            r = a + work[2 * k + j, :, :half]
            m = b + work[2 * k + j, :, half:]
            rs.append(r)
            ms.append(m)
        at = pl.ds(pl.multiple_of(k * 16, 16), 16)
        st_b[at, :half] = jnp.concatenate(rs, axis=0).astype(BF16)
        st_b[at, half:] = jnp.concatenate(ms, axis=0).astype(BF16)
        return r, m

    lax.fori_loop(0, group // 2, state_step, (sr0, si0))

    swaps = []
    for k in range(n_out):
        at = pl.ds(k * COLS, COLS)
        val = jnp.dot(st_b[...], outm[:, at], preferred_element_type=F32)
        d_out[k] = val - tgt8[:, :, at].reshape(lines, COLS)
        swap = remote(d_out.at[k], d_in.at[k], pair_send.at[1 + k], pair_recv.at[1 + k], mate)
        swap.start()
        swaps.append(swap)

    def grad(k, left, right):
        for i in range(width // COLS):
            val = lax.dot_general(
                left[:, pl.ds(i * COLS, COLS)], right, (((0,), (0,)), ((), ())),
                preferred_element_type=F32,
            )
            if rows >= COLS:
                per = rows // COLS
                q = i // per
                gp[k, q // nb, q % nb, pl.ds((i % per) * COLS, COLS), :] = val
            else:
                for j in range(COLS // rows):
                    q = i * (COLS // rows) + j
                    gp[k, q // nb, q % nb] = val[j * rows : (j + 1) * rows]

    def a_dev(a):
        return (a * nb + pb) * 2 + core

    def b_dev(b):
        return (pa * nb + b) * 2 + core

    first_a = Chain(na, pa, a_dev, lambda c: gp.at[0, c], zz, zzsend, zzrecv)
    then_b = Chain(nb, pb, b_dev, lambda c: gp.at[0, pa, c], zy, zysend, zyrecv)
    bs = [
        Chain(nb, pb, b_dev, lambda c, k=k: gp.at[k, :, c], ys.at[k - 1], ysend.at[k - 1], yrecv.at[k - 1])
        for k in range(1, n_out + 1)
    ]
    as_ = [
        Chain(na, pa, a_dev, lambda c, k=k: gp.at[k, c, pb], zs.at[k - 1], zsend.at[k - 1], zrecv.at[k - 1])
        for k in range(1, n_out + 1)
    ]

    def run(chain, lo, hi):
        if chain.n > 2:

            def body(s, _):
                chain.step(s)
                return 0

            lax.fori_loop(lo, hi, body, 0)

    for k in range(n_out):
        swaps[k].wait()
        mis[:, k * COLS : (k + 1) * COLS] = (d_out[k] + d_in[k]).astype(BF16)
        grad(k, st_b, mis[:, k * COLS : (k + 1) * COLS])
        if k == 0:
            first_a.lead()
        else:
            bs[k - 1].lead()

    def back_block(i, _):
        at = pl.ds(pl.multiple_of(i * COLS, COLS), COLS)
        val = lax.dot_general(
            mis[...], outm[at, :], (((1,), (1,)), ((), ())), preferred_element_type=F32
        )
        work[:, :, at] = val.reshape(group, 8, COLS)
        return 0

    lax.fori_loop(0, width // COLS, back_block, 0)

    def cmulc(ar, ai, br, bi):
        return ar * br + ai * bi, ar * bi - ai * br

    def starts_step(k, carry):
        t = group - 1 - k
        r, m = carry
        a, b = cmulc(pole_ref[0], pole_ref[1], r, m)
        return a + work[t, :, :half], b + work[t, :, half:]

    br_, bi_ = lax.fori_loop(0, group, starts_step, (zero, zero), unroll=2)
    cr, ci = cmulc(g4r, g4i, br_[4:], bi_[4:])
    f_out[:4, :] = cr + br_[:4]
    f_out[4:, :] = ci + bi_[:4]

    def send_rev(q, _):
        remote(f_out, f_in.at[chip], fs.at[q], fr.at[chip], q * 2 + core).start()
        return 0

    lax.fori_loop(0, chip, send_rev, 0)
    first_a.pass_on(0, True)

    def take_rev(k, carry):
        q = chips - 1 - k
        r, m = carry
        remote(f_out, f_in.at[q], fs.at[q], fr.at[q], mate).wait_recv()
        a, b = cmulc(h4r, h4i, r, m)
        return a + f_in[q, :4, :], b + f_in[q, 4:, :]

    xr, xi = lax.fori_loop(0, chips - 1 - chip, take_rev, (z4, z4))
    ur, ui = cmulc(g4r, g4i, xr, xi)
    ar0 = jnp.concatenate([ur + br_[4:], xr], axis=0)
    ai0 = jnp.concatenate([ui + bi_[4:], xi], axis=0)

    def adj_step(k, carry):
        r, m = carry
        k2 = group // 2 - 1 - k
        rs, ms = [], []
        for j in (1, 0):
            a, b = cmulc(pole_ref[0], pole_ref[1], r, m)
            r = a + work[2 * k2 + j, :, :half]
            m = b + work[2 * k2 + j, :, half:]
            rs.insert(0, r * gain_ref[:, :half])
            ms.insert(0, m * gain_ref[:, half:])
        at = pl.ds(pl.multiple_of(k2 * 16, 16), 16)
        ad_b[at, :half] = jnp.concatenate(rs, axis=0).astype(BF16)
        ad_b[at, half:] = jnp.concatenate(ms, axis=0).astype(BF16)
        return r, m

    ar_, ai_ = lax.fori_loop(0, group // 2, adj_step, (ar0, ai0))
    bnd_ref[:, :half] = ar_ * gain_ref[:, :half]
    bnd_ref[:, half:] = ai_ * gain_ref[:, half:]
    bnd_copy = remote(
        bnd_ref, bnr_ref, pair_send.at[1 + n_out], pair_recv.at[1 + n_out], mate
    )
    bnd_copy.start()

    grad(n_out, ad_b, sig_b[...])

    bs[n_out - 1].lead()
    first_a.pass_on(0, False)
    for k in range(n_out):
        if k == 0:
            run(first_a, 1, na - 1)
        run(bs[k], 0, nb - 1)
        bs[k].finish()
        as_[k].lead()
        if k == 0:
            first_a.finish()
            then_b.lead()
        else:
            as_[k - 1].finish()
        run(as_[k], 0, na - 1)
    run(then_b, 0, nb - 1)
    then_b.finish()
    as_[n_out - 1].finish()

    def part(x):
        v = jnp.sum((x * x).reshape(rows // 8, 8, COLS), axis=0)
        return v[:, :128] + v[:, 128:]

    total = part(gp[0, pa, pb])
    for k in range(1, n_out):
        total = total + part(gp[k, pa, pb])
    sq_out[0] = total
    sq_out[1] = part(gp[n_out, pa, pb])

    def send_sq(k, _):
        other = (me + k) % n_tm
        remote(sq_out, sq_in.at[me], qs.at[other], qr.at[me], other).start()
        return 0

    lax.fori_loop(1, n_tm, send_sq, 0)
    sq_in[me] = sq_out[...]

    def take_sq(k, _):
        other = (me + k) % n_tm
        remote(sq_out, sq_in.at[other], qs.at[other], qr.at[other], other).wait_recv()
        return 0

    lax.fori_loop(1, n_tm, take_sq, 0)
    sums = jnp.sum(sq_in[...], axis=0)
    count = 2.0 * width
    out_scale = lax.rsqrt(jnp.sum(sums[0], keepdims=True) / (count * COLS * n_out) + 1e-6)
    in_scale = lax.rsqrt(jnp.sum(sums[1], keepdims=True) / (count * COLS) + 1e-6)
    for k in range(n_out):
        upd_ref[:, k * COLS : (k + 1) * COLS] = gp[k, pa, pb] * out_scale
    upi_ref[...] = gp[n_out, pa, pb] * in_scale

    def sent_sq(k, _):
        other = (me + k) % n_tm
        remote(sq_out, sq_in.at[me], qs.at[other], qr.at[me], other).wait_send()
        return 0

    lax.fori_loop(1, n_tm, sent_sq, 0)

    def sent_fwd(q, _):
        remote(e_out, e_in.at[chip], es.at[q], er.at[chip], q * 2 + core).wait_send()
        return 0

    lax.fori_loop(chip + 1, chips, sent_fwd, 0)

    def sent_rev(q, _):
        remote(f_out, f_in.at[chip], fs.at[q], fr.at[chip], q * 2 + core).wait_send()
        return 0

    lax.fori_loop(0, chip, sent_rev, 0)
    bnd_copy.wait()
    for chain in [first_a, then_b] + bs + as_:
        chain.drain()


def per_device(na, nb, signals, targets, decay_rate, pole_angle, in_map, out_map):
    members, group, sensors = signals.shape
    modes = decay_rate.shape[0]
    chips = na * nb
    rows = in_map.shape[0] // (2 * chips)
    core = lax.axis_index("tm") % 2
    half = modes // 2
    width = modes
    n_out = out_map.shape[1] // COLS
    lines = 2 * members * group

    def own(x):
        return lax.dynamic_index_in_dim(x.reshape(-1, 2, rows), core, 1, False).reshape(half)

    rate, angle = own(decay_rate), own(pole_angle)
    size = jnp.exp(-rate)
    pole = jnp.stack([size * jnp.cos(angle), size * jnp.sin(angle)])
    pole = pole[:, None, :]
    gain = jnp.sqrt(-jnp.expm1(-2.0 * rate))
    gain = jnp.concatenate([gain, gain])[None]

    vm = pl.BlockSpec(memory_space=pltpu.VMEM)
    anyw = pl.BlockSpec(memory_space=pl.ANY)
    dma = pltpu.SemaphoreType.DMA
    scratch = [
        pltpu.VMEM((width, sensors), BF16),
        pltpu.VMEM((width, n_out * COLS), BF16),
        pltpu.VMEM((group, 8, sensors), F32),
        pltpu.VMEM((lines, sensors), BF16),
        pltpu.VMEM((group, 8, width), F32),
        pltpu.VMEM((lines, width), BF16),
        pltpu.VMEM((lines, width), BF16),
        pltpu.VMEM((n_out, lines, COLS), F32),
        pltpu.VMEM((n_out, lines, COLS), F32),
        pltpu.VMEM((lines, n_out * COLS), BF16),
        pltpu.VMEM((8, half), F32),
        pltpu.VMEM((chips, 8, half), F32),
        pltpu.VMEM((8, half), F32),
        pltpu.VMEM((chips, 8, half), F32),
        pltpu.VMEM((2, 8, 128), F32),
        pltpu.VMEM((2 * chips, 2, 8, 128), F32),
        pltpu.VMEM((n_out + 1, na, nb, rows, COLS), F32),
        pltpu.VMEM((n_out, nb + 1, na, rows, COLS), F32),
        pltpu.VMEM((n_out, na + 1, rows, COLS), F32),
        pltpu.VMEM((na + 1, nb, rows, COLS), F32),
        pltpu.VMEM((nb + 1, rows, COLS), F32),
        pltpu.VMEM((group, 8, sensors), F32),
        pltpu.VMEM((group, 8, n_out * COLS), F32),
        pltpu.VMEM((2, 8, half), F32),
        dma((2, chips)),
        dma((n_out + 2,)),
        dma((n_out + 2,)),
        dma((chips,)),
        dma((chips,)),
        dma((chips,)),
        dma((chips,)),
        dma((2 * chips,)),
        dma((2 * chips,)),
        dma((n_out, nb)),
        dma((n_out, nb + 1)),
        dma((n_out, na)),
        dma((n_out, na + 1)),
        dma((na,)),
        dma((na + 1,)),
        dma((nb,)),
        dma((nb + 1,)),
    ]
    upd, upi, bnd, bnr = pl.pallas_call(
        functools.partial(kernel, na, nb, group, rows),
        out_shape=(
            jax.ShapeDtypeStruct((rows, n_out * COLS), F32),
            jax.ShapeDtypeStruct((rows, sensors), F32),
            jax.ShapeDtypeStruct((8, width), F32),
            jax.ShapeDtypeStruct((8, width), F32),
        ),
        in_specs=[vm, vm, vm, vm, anyw, anyw],
        out_specs=(vm, vm, vm, vm),
        scratch_shapes=scratch,
        compiler_params=pltpu.CompilerParams(
            collective_id=0, has_side_effects=True, vmem_limit_bytes=62 * 1024 * 1024
        ),
    )(
        signals,
        targets,
        pole,
        gain,
        in_map.reshape(chips, 2, rows, sensors),
        out_map.reshape(chips, 2, rows, n_out * COLS),
    )
    bnd = lax.dynamic_slice_in_dim(bnd, core * members, members, 0).reshape(members, chips, rows)
    bnr = lax.dynamic_slice_in_dim(bnr, core * members, members, 0).reshape(members, chips, rows)
    even = jnp.where(core == 0, bnd, bnr)
    odd = jnp.where(core == 0, bnr, bnd)
    boundary = jnp.stack([even, odd], axis=2).reshape(members, 1, 2 * width)
    return upd, upi, boundary


def solution(mesh):
    chips = mesh.shape["tm"] // 2
    nb = 1
    while 4 * nb * nb <= chips:
        nb *= 2
    na = chips // nb
    return jax.shard_map(
        functools.partial(per_device, na, nb),
        mesh=mesh,
        in_specs=(
            P("grp", "tm", None),
            P("grp", "tm", None),
            P("grp"),
            P("grp"),
            P("grp", None),
            P("grp", None),
        ),
        out_specs=(P(("grp", "tm"), None), P(("grp", "tm"), None), P("grp", "tm", None)),
        check_vma=False,
    )
```

```python
import functools

import jax
import jax.numpy as jnp
from jax import lax
from jax.experimental import pallas as pl
from jax.experimental.pallas import tpu as pltpu
from jax.sharding import PartitionSpec as P

F32 = jnp.float32
BF16 = jnp.bfloat16
MESH = pl.DeviceIdType.MESH
COLS = 256


def remote(src, dst, send_sem, recv_sem, device):
    return pltpu.make_async_remote_copy(
        src_ref=src,
        dst_ref=dst,
        send_sem=send_sem,
        recv_sem=recv_sem,
        device_id={"tm": device},
        device_id_type=MESH,
    )


def cmul(ar, ai, br, bi):
    return ar * br - ai * bi, ar * bi + ai * br


class Chain:
    def __init__(self, n, pos, device_of, chunk, slots, send, recv):
        self.n, self.pos, self.device_of, self.chunk = n, pos, device_of, chunk
        self.slots, self.send, self.recv = slots, send, recv

    def copy(self, c, slot, to):
        return remote(
            self.chunk(c), self.slots.at[slot], self.send.at[c], self.recv.at[slot], self.device_of(to)
        )

    def arrive(self, slot):
        self.copy(slot % self.n, slot, self.pos).wait_recv()

    def launch(self, c, right):
        to = jnp.where(right, self.pos + 1, self.pos - 1)
        slot = jnp.where(jnp.logical_and(jnp.logical_not(right), c == self.pos - 1), self.n, c)
        self.copy(c, slot, to).start()

    def lead(self):
        n, p = self.n, self.pos

        @pl.when(jnp.logical_or(p == 0, p == n - 1))
        def _():
            def body(s, _):
                right = p == 0
                self.launch(jnp.where(right, n - 1 - s, s), right)
                return 0

            lax.fori_loop(0, n - 1, body, 0)

    def pass_on(self, s, first):
        n, p = self.n, self.pos
        low = 2 * p < n
        right = low if first else jnp.logical_not(low)
        c = jnp.where(right, n - 1 - s, s)
        go = jnp.where(right, jnp.logical_and(c > p, p > 0), jnp.logical_and(c < p, p < n - 1))

        @pl.when(go)
        def _():
            self.arrive(c)
            mine = self.chunk(c)
            mine[...] = mine[...] + self.slots[c]
            self.launch(c, right)

    def step(self, s):
        if self.n > 2:
            self.pass_on(s, True)
            self.pass_on(s, False)

    def finish(self):
        n, p = self.n, self.pos
        mine = self.chunk(p)

        @pl.when(p > 0)
        def _():
            self.arrive(p)
            mine[...] = mine[...] + self.slots[p]

        @pl.when(p < n - 1)
        def _():
            self.arrive(n)
            mine[...] = mine[...] + self.slots[n]

    def drain(self):
        for c in range(self.n):

            @pl.when(self.pos != c)
            def _():
                self.copy(c, c, self.pos).wait_send()


def kernel(
    na, nb, group, rows,
    sig_ref, tgt_ref, pole_row, gain_ref, in_hbm, out_hbm,
    upd_ref, upi_ref, bnd_ref, bnr_ref,
    inm, outm, sig_in, sig_b, work, st_b, ad_b, d_out, d_in, mis,
    e_out, e_in, f_out, f_in, sq_out, sq_in,
    gp, ys, zs, zz, zy, sig8, tgt8, pole_ref,
    ld_sem, pair_send, pair_recv, es, er, fs, fr, qs, qr,
    ysend, yrecv, zsend, zrecv, zzsend, zzrecv, zysend, zyrecv,
):
    chips = na * nb
    n_tm = 2 * chips
    me = lax.axis_index("tm")
    core = me % 2
    chip = me // 2
    pa = chip // nb
    pb = chip % nb
    mate = chip * 2 + 1 - core
    half = pole_row.shape[2]
    width = 2 * half
    lines = 8 * group
    n_out = outm.shape[1] // COLS

    loads = []
    for q in range(chips):
        loads.append(
            pltpu.make_async_copy(in_hbm.at[q, core], inm.at[pl.ds(q * rows, rows)], ld_sem.at[0, q])
        )
        loads.append(
            pltpu.make_async_copy(out_hbm.at[q, core], outm.at[pl.ds(q * rows, rows)], ld_sem.at[1, q])
        )
    for load in loads:
        load.start()

    def interleave(wide, x_ref):
        wide[...] = jnp.zeros(wide.shape, F32)
        for c in range(2):

            @pl.when(core == c)
            def _():
                for m in range(4):
                    wide[:, 4 * c + m, :] = x_ref[m].astype(F32)

    interleave(sig8, sig_ref)
    pole_ref[...] = jnp.broadcast_to(pole_row[...], pole_ref.shape)

    barrier = pltpu.get_barrier_semaphore()

    def greet(k, _):
        other = (me + k) % n_tm
        pl.semaphore_signal(barrier, inc=1, device_id={"tm": other}, device_id_type=MESH)
        return 0

    lax.fori_loop(1, n_tm, greet, 0)
    pl.semaphore_wait(barrier, n_tm - 1)

    sig_copy = remote(sig8, sig_in, pair_send.at[0], pair_recv.at[0], mate)
    sig_copy.start()
    for load in loads[0::2]:
        load.wait()
    sig_copy.wait()
    sig_b[...] = (sig8[...] + sig_in[...]).reshape(sig_b.shape).astype(BF16)

    def drive_block(i, _):
        at = pl.ds(pl.multiple_of(i * COLS, COLS), COLS)
        val = lax.dot_general(
            sig_b[...], inm[at, :], (((1,), (1,)), ((), ())), preferred_element_type=F32
        )
        work[:, :, at] = val.reshape(group, 8, COLS) * gain_ref[:, at][None]
        return 0

    lax.fori_loop(0, width // COLS, drive_block, 0)

    pr = pole_ref[0]
    pi = pole_ref[1]
    gr, gi = pr, pi
    span = 1
    while span < group:
        gr, gi = cmul(gr, gi, gr, gi)
        span *= 2
    hr, hi = cmul(gr, gi, gr, gi)
    g4r, g4i, h4r, h4i = gr[:4], gi[:4], hr[:4], hi[:4]
    zero = jnp.zeros((8, half), F32)

    def ends_step(t, carry):
        r, m = carry
        a, b = cmul(pole_ref[0], pole_ref[1], r, m)
        return a + work[t, :, :half], b + work[t, :, half:]

    er_, ei_ = lax.fori_loop(0, group, ends_step, (zero, zero), unroll=2)
    cr, ci = cmul(g4r, g4i, er_[:4], ei_[:4])
    e_out[:4, :] = cr + er_[4:]
    e_out[4:, :] = ci + ei_[4:]

    def send_fwd(q, _):
        remote(e_out, e_in.at[chip], es.at[q], er.at[chip], q * 2 + core).start()
        return 0

    lax.fori_loop(chip + 1, chips, send_fwd, 0)
    interleave(tgt8, tgt_ref)

    def take_fwd(q, carry):
        r, m = carry
        remote(e_out, e_in.at[q], es.at[q], er.at[q], mate).wait_recv()
        a, b = cmul(h4r, h4i, r, m)
        return a + e_in[q, :4, :], b + e_in[q, 4:, :]

    z4 = jnp.zeros((4, half), F32)
    xr, xi = lax.fori_loop(0, chip, take_fwd, (z4, z4))
    ur, ui = cmul(g4r, g4i, xr, xi)
    sr0 = jnp.concatenate([xr, ur + er_[:4]], axis=0)
    si0 = jnp.concatenate([xi, ui + ei_[:4]], axis=0)

    def state_step(k, carry):
        r, m = carry
        rs, ms = [], []
        for j in range(2):
            a, b = cmul(pole_ref[0], pole_ref[1], r, m)
            r = a + work[2 * k + j, :, :half]
            m = b + work[2 * k + j, :, half:]
            rs.append(r)
            ms.append(m)
        at = pl.ds(pl.multiple_of(k * 16, 16), 16)
        st_b[at, :half] = jnp.concatenate(rs, axis=0).astype(BF16)
        st_b[at, half:] = jnp.concatenate(ms, axis=0).astype(BF16)
        return r, m

    lax.fori_loop(0, group // 2, state_step, (sr0, si0))

    for load in loads[1::2]:
        load.wait()

    swaps = []
    for k in range(n_out):
        at = pl.ds(k * COLS, COLS)
        val = jnp.dot(st_b[...], outm[:, at], preferred_element_type=F32)
        d_out[k] = val - tgt8[:, :, at].reshape(lines, COLS)
        swap = remote(d_out.at[k], d_in.at[k], pair_send.at[1 + k], pair_recv.at[1 + k], mate)
        swap.start()
        swaps.append(swap)

    def grad(k, left, right):
        for i in range(width // COLS):
            val = lax.dot_general(
                left[:, pl.ds(i * COLS, COLS)], right, (((0,), (0,)), ((), ())),
                preferred_element_type=F32,
            )
            if rows >= COLS:
                per = rows // COLS
                q = i // per
                gp[k, q // nb, q % nb, pl.ds((i % per) * COLS, COLS), :] = val
            else:
                for j in range(COLS // rows):
                    q = i * (COLS // rows) + j
                    gp[k, q // nb, q % nb] = val[j * rows : (j + 1) * rows]

    def a_dev(a):
        return (a * nb + pb) * 2 + core

    def b_dev(b):
        return (pa * nb + b) * 2 + core

    first_a = Chain(na, pa, a_dev, lambda c: gp.at[0, c], zz, zzsend, zzrecv)
    then_b = Chain(nb, pb, b_dev, lambda c: gp.at[0, pa, c], zy, zysend, zyrecv)
    bs = [
        Chain(nb, pb, b_dev, lambda c, k=k: gp.at[k, :, c], ys.at[k - 1], ysend.at[k - 1], yrecv.at[k - 1])
        for k in range(1, n_out + 1)
    ]
    as_ = [
        Chain(na, pa, a_dev, lambda c, k=k: gp.at[k, c, pb], zs.at[k - 1], zsend.at[k - 1], zrecv.at[k - 1])
        for k in range(1, n_out + 1)
    ]

    def run(chain, lo, hi):
        if chain.n > 2:

            def body(s, _):
                chain.step(s)
                return 0

            lax.fori_loop(lo, hi, body, 0)

    for k in range(n_out):
        swaps[k].wait()
        mis[:, k * COLS : (k + 1) * COLS] = (d_out[k] + d_in[k]).astype(BF16)
        grad(k, st_b, mis[:, k * COLS : (k + 1) * COLS])
        if k == 0:
            first_a.lead()
        else:
            bs[k - 1].lead()

    def back_block(i, _):
        at = pl.ds(pl.multiple_of(i * COLS, COLS), COLS)
        val = lax.dot_general(
            mis[...], outm[at, :], (((1,), (1,)), ((), ())), preferred_element_type=F32
        )
        work[:, :, at] = val.reshape(group, 8, COLS)
        return 0

    lax.fori_loop(0, width // COLS, back_block, 0)

    def cmulc(ar, ai, br, bi):
        return ar * br + ai * bi, ar * bi - ai * br

    def starts_step(k, carry):
        t = group - 1 - k
        r, m = carry
        a, b = cmulc(pole_ref[0], pole_ref[1], r, m)
        return a + work[t, :, :half], b + work[t, :, half:]

    br_, bi_ = lax.fori_loop(0, group, starts_step, (zero, zero), unroll=2)
    cr, ci = cmulc(g4r, g4i, br_[4:], bi_[4:])
    f_out[:4, :] = cr + br_[:4]
    f_out[4:, :] = ci + bi_[:4]

    def send_rev(q, _):
        remote(f_out, f_in.at[chip], fs.at[q], fr.at[chip], q * 2 + core).start()
        return 0

    lax.fori_loop(0, chip, send_rev, 0)
    first_a.pass_on(0, True)

    def take_rev(k, carry):
        q = chips - 1 - k
        r, m = carry
        remote(f_out, f_in.at[q], fs.at[q], fr.at[q], mate).wait_recv()
        a, b = cmulc(h4r, h4i, r, m)
        return a + f_in[q, :4, :], b + f_in[q, 4:, :]

    xr, xi = lax.fori_loop(0, chips - 1 - chip, take_rev, (z4, z4))
    ur, ui = cmulc(g4r, g4i, xr, xi)
    ar0 = jnp.concatenate([ur + br_[4:], xr], axis=0)
    ai0 = jnp.concatenate([ui + bi_[4:], xi], axis=0)

    def adj_step(k, carry):
        r, m = carry
        k2 = group // 2 - 1 - k
        rs, ms = [], []
        for j in (1, 0):
            a, b = cmulc(pole_ref[0], pole_ref[1], r, m)
            r = a + work[2 * k2 + j, :, :half]
            m = b + work[2 * k2 + j, :, half:]
            rs.insert(0, r * gain_ref[:, :half])
            ms.insert(0, m * gain_ref[:, half:])
        at = pl.ds(pl.multiple_of(k2 * 16, 16), 16)
        ad_b[at, :half] = jnp.concatenate(rs, axis=0).astype(BF16)
        ad_b[at, half:] = jnp.concatenate(ms, axis=0).astype(BF16)
        return r, m

    ar_, ai_ = lax.fori_loop(0, group // 2, adj_step, (ar0, ai0))
    bnd_ref[:, :half] = ar_ * gain_ref[:, :half]
    bnd_ref[:, half:] = ai_ * gain_ref[:, half:]
    bnd_copy = remote(
        bnd_ref, bnr_ref, pair_send.at[1 + n_out], pair_recv.at[1 + n_out], mate
    )
    bnd_copy.start()

    grad(n_out, ad_b, sig_b[...])

    bs[n_out - 1].lead()
    first_a.pass_on(0, False)
    for k in range(n_out):
        if k == 0:
            run(first_a, 1, na - 1)
        run(bs[k], 0, nb - 1)
        bs[k].finish()
        as_[k].lead()
        if k == 0:
            first_a.finish()
            then_b.lead()
        else:
            as_[k - 1].finish()
        run(as_[k], 0, na - 1)
    run(then_b, 0, nb - 1)
    then_b.finish()
    as_[n_out - 1].finish()

    def part(x):
        v = jnp.sum((x * x).reshape(rows // 8, 8, COLS), axis=0)
        return v[:, :128] + v[:, 128:]

    total = part(gp[0, pa, pb])
    for k in range(1, n_out):
        total = total + part(gp[k, pa, pb])
    sq_out[0] = total
    sq_out[1] = part(gp[n_out, pa, pb])

    def send_sq(k, _):
        other = (me + k) % n_tm
        remote(sq_out, sq_in.at[me], qs.at[other], qr.at[me], other).start()
        return 0

    lax.fori_loop(1, n_tm, send_sq, 0)
    sq_in[me] = sq_out[...]

    def take_sq(k, _):
        other = (me + k) % n_tm
        remote(sq_out, sq_in.at[other], qs.at[other], qr.at[other], other).wait_recv()
        return 0

    lax.fori_loop(1, n_tm, take_sq, 0)
    sums = jnp.sum(sq_in[...], axis=0)
    count = 2.0 * width
    out_scale = lax.rsqrt(jnp.sum(sums[0], keepdims=True) / (count * COLS * n_out) + 1e-6)
    in_scale = lax.rsqrt(jnp.sum(sums[1], keepdims=True) / (count * COLS) + 1e-6)
    for k in range(n_out):
        upd_ref[:, k * COLS : (k + 1) * COLS] = gp[k, pa, pb] * out_scale
    upi_ref[...] = gp[n_out, pa, pb] * in_scale

    def sent_sq(k, _):
        other = (me + k) % n_tm
        remote(sq_out, sq_in.at[me], qs.at[other], qr.at[me], other).wait_send()
        return 0

    lax.fori_loop(1, n_tm, sent_sq, 0)

    def sent_fwd(q, _):
        remote(e_out, e_in.at[chip], es.at[q], er.at[chip], q * 2 + core).wait_send()
        return 0

    lax.fori_loop(chip + 1, chips, sent_fwd, 0)

    def sent_rev(q, _):
        remote(f_out, f_in.at[chip], fs.at[q], fr.at[chip], q * 2 + core).wait_send()
        return 0

    lax.fori_loop(0, chip, sent_rev, 0)
    bnd_copy.wait()
    for chain in [first_a, then_b] + bs + as_:
        chain.drain()


def per_device(na, nb, signals, targets, decay_rate, pole_angle, in_map, out_map):
    members, group, sensors = signals.shape
    modes = decay_rate.shape[0]
    chips = na * nb
    rows = in_map.shape[0] // (2 * chips)
    core = lax.axis_index("tm") % 2
    half = modes // 2
    width = modes
    n_out = out_map.shape[1] // COLS
    lines = 2 * members * group

    def own(x):
        return lax.dynamic_index_in_dim(x.reshape(-1, 2, rows), core, 1, False).reshape(half)

    rate, angle = own(decay_rate), own(pole_angle)
    size = jnp.exp(-rate)
    pole = jnp.stack([size * jnp.cos(angle), size * jnp.sin(angle)])
    pole = pole[:, None, :]
    gain = jnp.sqrt(-jnp.expm1(-2.0 * rate))
    gain = jnp.concatenate([gain, gain])[None]

    vm = pl.BlockSpec(memory_space=pltpu.VMEM)
    anyw = pl.BlockSpec(memory_space=pl.ANY)
    dma = pltpu.SemaphoreType.DMA
    scratch = [
        pltpu.VMEM((width, sensors), BF16),
        pltpu.VMEM((width, n_out * COLS), BF16),
        pltpu.VMEM((group, 8, sensors), F32),
        pltpu.VMEM((lines, sensors), BF16),
        pltpu.VMEM((group, 8, width), F32),
        pltpu.VMEM((lines, width), BF16),
        pltpu.VMEM((lines, width), BF16),
        pltpu.VMEM((n_out, lines, COLS), F32),
        pltpu.VMEM((n_out, lines, COLS), F32),
        pltpu.VMEM((lines, n_out * COLS), BF16),
        pltpu.VMEM((8, half), F32),
        pltpu.VMEM((chips, 8, half), F32),
        pltpu.VMEM((8, half), F32),
        pltpu.VMEM((chips, 8, half), F32),
        pltpu.VMEM((2, 8, 128), F32),
        pltpu.VMEM((2 * chips, 2, 8, 128), F32),
        pltpu.VMEM((n_out + 1, na, nb, rows, COLS), F32),
        pltpu.VMEM((n_out, nb + 1, na, rows, COLS), F32),
        pltpu.VMEM((n_out, na + 1, rows, COLS), F32),
        pltpu.VMEM((na + 1, nb, rows, COLS), F32),
        pltpu.VMEM((nb + 1, rows, COLS), F32),
        pltpu.VMEM((group, 8, sensors), F32),
        pltpu.VMEM((group, 8, n_out * COLS), F32),
        pltpu.VMEM((2, 8, half), F32),
        dma((2, chips)),
        dma((n_out + 2,)),
        dma((n_out + 2,)),
        dma((chips,)),
        dma((chips,)),
        dma((chips,)),
        dma((chips,)),
        dma((2 * chips,)),
        dma((2 * chips,)),
        dma((n_out, nb)),
        dma((n_out, nb + 1)),
        dma((n_out, na)),
        dma((n_out, na + 1)),
        dma((na,)),
        dma((na + 1,)),
        dma((nb,)),
        dma((nb + 1,)),
    ]
    upd, upi, bnd, bnr = pl.pallas_call(
        functools.partial(kernel, na, nb, group, rows),
        out_shape=(
            jax.ShapeDtypeStruct((rows, n_out * COLS), F32),
            jax.ShapeDtypeStruct((rows, sensors), F32),
            jax.ShapeDtypeStruct((8, width), F32),
            jax.ShapeDtypeStruct((8, width), F32),
        ),
        in_specs=[vm, vm, vm, vm, anyw, anyw],
        out_specs=(vm, vm, vm, vm),
        scratch_shapes=scratch,
        compiler_params=pltpu.CompilerParams(
            collective_id=0, has_side_effects=True, vmem_limit_bytes=62 * 1024 * 1024
        ),
    )(
        signals,
        targets,
        pole,
        gain,
        in_map.reshape(chips, 2, rows, sensors),
        out_map.reshape(chips, 2, rows, n_out * COLS),
    )
    bnd = lax.dynamic_slice_in_dim(bnd, core * members, members, 0).reshape(members, chips, rows)
    bnr = lax.dynamic_slice_in_dim(bnr, core * members, members, 0).reshape(members, chips, rows)
    even = jnp.where(core == 0, bnd, bnr)
    odd = jnp.where(core == 0, bnr, bnd)
    boundary = jnp.stack([even, odd], axis=2).reshape(members, 1, 2 * width)
    return upd, upi, boundary


def solution(mesh):
    chips = mesh.shape["tm"] // 2
    nb = 1
    while 4 * nb * nb <= chips:
        nb *= 2
    na = chips // nb
    return jax.shard_map(
        functools.partial(per_device, na, nb),
        mesh=mesh,
        in_specs=(
            P("grp", "tm", None),
            P("grp", "tm", None),
            P("grp"),
            P("grp"),
            P("grp", None),
            P("grp", None),
        ),
        out_specs=(P(("grp", "tm"), None), P(("grp", "tm"), None), P("grp", "tm", None)),
        check_vma=False,
    )
```
